128 devices in a mesh: rows: 128 (over x, y, z, core).
Axes of the slice: x: 4, y: 4, z: 4, core: 2. Of those that a mesh axis runs over, the one named last changes fastest.
Arguments:
- tokens: float32 [128, 1024, 256], P('rows'), may hold values from -6 to 6
- stored: float32 [128, 1024, 256], P('rows'), may hold values from -6 to 6
- upstream: float32 [128, 1024, 256], P('rows'), may hold values from -6 to 6
- drop_attn: int32 [128, 14, 1024], P('rows'), may hold values from 0 to 524287
- drop_ffn: int32 [128, 14, 1024], P('rows'), may hold values from 0 to 524287
- depth_keep: int32 [2, 16, 128], replicated, may hold values 0 or 1
- gain_one: float32 [256], replicated, may hold values from 0.1 to 1.9
- shift_one: float32 [256], replicated, may hold values from -3 to 3
- w_qkv: float32 [256, 768], replicated, as said below
- w_out: float32 [256, 256], replicated, may hold values from -0.375 to 0.375
- gain_two: float32 [256], replicated, may hold values from 0.1 to 1.9
- shift_two: float32 [256], replicated, may hold values from -3 to 3
- w_up: float32 [256, 1024], replicated, may hold values from -0.375 to 0.375
- up_bias: float32 [1024], replicated, may hold values from -3 to 3
- w_down: float32 [1024, 256], replicated, may hold values from -0.1875 to 0.1875
Outputs:
- result: float32 [128, 1024, 256], P('rows')
- grad_gain_one: float32 [256], replicated
- grad_shift_one: float32 [256], replicated
- grad_w_qkv: float32 [256, 768], replicated
- grad_w_out: float32 [256, 256], replicated
- grad_gain_two: float32 [256], replicated
- grad_shift_two: float32 [256], replicated
- grad_w_up: float32 [256, 1024], replicated
- grad_up_bias: float32 [1024], replicated
- grad_w_down: float32 [1024, 256], replicated
The draws below stay inside these ranges and needn't reach their ends.
Inputs may be any that keep to these rules, and one draw needn't show every extreme that they name: `w_qkv`: columns are the queries, then the keys, then the values, each head's 32 columns together.
All inputs are finite; a program needn't handle non-finite values.
Results may differ from the reference program's by a relative error of at most 0.0003.
Values sent between devices are 32-bit elements; how exact they have to be, the bound alone decides.
A program may use at most 384 MiB of HBM per device.

```python
import jax
import jax.numpy as jnp
from jax import lax

D = 256
NH = 8
FF = 1024
MAP_COLS = 1024
MAP_ROWS = 128
TOKENS = 131072
NWORD = 14


def draw_w_qkv(key, part):
    key = jax.random.fold_in(key, 7)
    matrix = jax.random.normal(jax.random.fold_in(key, 1), (D, 3 * D), jnp.float32) * D ** (-0.5)
    return matrix


def with_ends(values, stream_key, least, high):
    longest = values.shape.index(max(values.shape))
    spots = []
    for shift in (0, 1):
        where = [jax.random.randint(jax.random.fold_in(stream_key, axis), (), 0, length) for axis, length in enumerate(values.shape)]
        where[longest] = (where[longest] + shift) % values.shape[longest]
        spots.append(tuple(where))
    return values.at[spots[0]].set(least).at[spots[1]].set(high)


def block_scale(rng, extent, cuts, least, high):
    factor_of, own = 1.0, jax.random.fold_in(rng, 6)
    for axis_at, blocks in cuts:
        steps = jnp.exp(jax.random.uniform(jax.random.fold_in(own, axis_at), (blocks,), jnp.float32, least / len(cuts), high / len(cuts)))
        factor_of = factor_of * jnp.repeat(steps, extent[axis_at] // blocks).reshape([-1 if axis == axis_at else 1 for axis in range(len(extent))])
    return factor_of


def scatter_about(key, extent, deviation, reach, pieces=(), held_as=jnp.bfloat16):
    drawn = jax.random.normal(key, extent, jnp.float32) * deviation
    if len(pieces) > 0:
        drawn = block_scale(key, extent, pieces, -0.22, 0.18) * drawn
    return jnp.clip(drawn, min=-reach, max=reach).astype(held_as)


def setup_inputs(seed: int = 0) -> dict:
    splits = jax.random.split(jax.random.key(seed), 16)
    return {
        "tokens": scatter_about(splits[0], (MAP_ROWS, MAP_COLS, D), 1.0, 6.0, ((0, 128),), jnp.float32),
        "stored": scatter_about(splits[1], (MAP_ROWS, MAP_COLS, D), 1.0, 6.0, ((0, 128),), jnp.float32),
        "upstream": scatter_about(splits[2], (MAP_ROWS, MAP_COLS, D), 1.0, 6.0, ((0, 128),), jnp.float32),
        "drop_attn": with_ends(jax.random.randint(splits[3], (MAP_ROWS, NWORD, MAP_COLS), 0, 524288), jax.random.fold_in(splits[3], 1), 0, 524287).astype(jnp.int32),
        "drop_ffn": with_ends(jax.random.randint(splits[4], (MAP_ROWS, NWORD, MAP_COLS), 0, 524288), jax.random.fold_in(splits[4], 1), 0, 524287).astype(jnp.int32),
        "depth_keep": with_ends((jax.random.randint(splits[5], (2, MAP_ROWS // 8, MAP_COLS // 8), 0, 4) < 3).astype(jnp.int32), jax.random.fold_in(splits[5], 1), 0, 1),
        "gain_one": jnp.clip(1.0 + 0.18 * jax.random.normal(splits[6], (D,), jnp.float32), 0.1, 1.9),
        "shift_one": scatter_about(splits[7], (D,), 0.5, 3.0, (), jnp.float32),
        "w_qkv": draw_w_qkv(jax.random.fold_in(splits[15], 71), 0),
        "w_out": scatter_about(splits[9], (D, D), D ** -0.5, 0.375, (), jnp.float32),
        "gain_two": jnp.clip(1.0 + 0.18 * jax.random.normal(splits[10], (D,), jnp.float32), 0.1, 1.9),
        "shift_two": scatter_about(splits[11], (D,), 0.5, 3.0, (), jnp.float32),
        "w_up": scatter_about(splits[12], (D, FF), D ** -0.5, 0.375, (), jnp.float32),
        "up_bias": scatter_about(splits[13], (FF,), 0.5, 3.0, (), jnp.float32),
        "w_down": scatter_about(splits[14], (FF, D), FF ** -0.5, 0.1875, (), jnp.float32),
    }


PRECISE = lax.Precision.HIGHEST
EPSILON = 1e-05
KEEP_SCALE = 8.0 / 3.0

def layer_norm(inputs, scales, offsets):
    average = lax.optimization_barrier(jnp.mean(inputs, -1, keepdims=True))
    centred = inputs - average
    spread = lax.optimization_barrier(jnp.mean(centred * centred, -1, keepdims=True))
    return centred * lax.rsqrt(spread + EPSILON) * scales + offsets

def attend(queries, keys_in, values_in, layout):
    key_layout = layout.replace('i', 'k').replace('j', 'l')
    scores = jnp.einsum(layout + ',' + key_layout + '->abnijkl', queries, keys_in, precision=PRECISE)
    scores = scores * queries.shape[-1] ** (-0.5)
    score_shape = scores.shape
    weights = jax.nn.softmax(scores.reshape(score_shape[:5] + (-1,)), axis=-1).reshape(score_shape)
    return jnp.einsum('abnijkl,' + key_layout + '->' + layout, weights, values_in, precision=PRECISE)

def attention_branch(layout, grid_tokens, gain_one, shift_one, w_qkv, w_out):
    normed = layer_norm(grid_tokens, gain_one, shift_one)
    projected = jnp.einsum('...c,ce->...e', normed, w_qkv, precision=PRECISE)
    parts = projected.reshape(projected.shape[:-1] + (3, NH, w_qkv.shape[0] // NH))
    mixed = attend(parts[..., 0, :, :], parts[..., 1, :, :], parts[..., 2, :, :], layout)
    merged = mixed.reshape(mixed.shape[:-2] + (w_out.shape[0],))
    return jnp.einsum('...c,ce->...e', merged, w_out, precision=PRECISE)

def attention_map(tokens, gain_one, shift_one, w_qkv, w_out):
    map_rows, columns, channels = tokens.shape
    grid_tokens = tokens.reshape(8, map_rows // 8, 8, columns // 8, channels)
    output = attention_branch('iajbnd', grid_tokens, gain_one, shift_one, w_qkv, w_out)
    return output.reshape(map_rows, columns, channels)

def ffn_branch(stored, gain_two, shift_two, w_up, up_bias, w_down):
    normed = layer_norm(stored, gain_two, shift_two)
    hidden = jax.nn.gelu(jnp.einsum('...c,cf->...f', normed, w_up, precision=PRECISE) + up_bias, approximate=False)
    return jnp.einsum('...f,fc->...c', hidden, w_down, precision=PRECISE)

def unpack(packed, channels):
    channel_ids = jnp.arange(channels, dtype=jnp.int32)
    picked = jnp.take(packed, channel_ids // 19, axis=1)
    bit_values = jnp.right_shift(picked, (channel_ids % 19)[None, :, None]) & 1
    return jnp.transpose(bit_values, (0, 2, 1)).astype(jnp.float32)

def reference(tokens, stored, upstream, drop_attn, drop_ffn, depth_keep, gain_one, shift_one, w_qkv, w_out, gain_two, shift_two, w_up, up_bias, w_down):
    flags = jnp.repeat(jnp.repeat(depth_keep, 8, axis=1), 8, axis=2).astype(jnp.float32)
    factor_attn = unpack(drop_attn, D) * flags[0][:, :, None] * KEEP_SCALE
    factor_ffn = unpack(drop_ffn, D) * flags[1][:, :, None] * KEEP_SCALE
    grad_scale = float(TOKENS) ** (-0.5)
    ffn_value, ffn_back = jax.vjp(ffn_branch, stored, gain_two, shift_two, w_up, up_bias, w_down)
    ffn_grads = ffn_back(upstream * factor_ffn)
    through = upstream + ffn_grads[0]
    attn_value, attn_back = jax.vjp(attention_map, tokens, gain_one, shift_one, w_qkv, w_out)
    attn_grads = attn_back(through * factor_attn)
    result = through + attn_grads[0]
    return (result, attn_grads[1] * grad_scale, attn_grads[2] * grad_scale, attn_grads[3] * grad_scale, attn_grads[4] * grad_scale, ffn_grads[1] * grad_scale, ffn_grads[2] * grad_scale, ffn_grads[3] * grad_scale, ffn_grads[4] * grad_scale, ffn_grads[5] * grad_scale)
```

```python
from functools import partial

import jax
import jax.numpy as jnp
from jax import lax
from jax.experimental import pallas as pl
from jax.experimental.pallas import tpu as pltpu
from jax.sharding import PartitionSpec as P

NH = 8
HD = 32
D = 256
FF = 1024
EPSILON = 1e-05
KEEP_SCALE = 8.0 / 3.0
BITS = 19
BF = jnp.bfloat16
F32 = jnp.float32

NN = (((1,), (0,)), ((), ()))
NT = (((1,), (1,)), ((), ()))
TN = (((0,), (0,)), ((), ()))


def mm(a, b, dims):
    return lax.dot_general(a, b, dims, preferred_element_type=F32)


def split(x):
    high = x.astype(BF)
    return high, (x - high.astype(F32)).astype(BF)


def cat(parts, axis):
    return jnp.concatenate(parts, axis=axis)


def norm_stats(x):
    average = jnp.mean(x, -1, keepdims=True)
    centred = x - average
    spread = jnp.mean(centred * centred, -1, keepdims=True)
    inverse = lax.rsqrt(spread + EPSILON)
    return centred * inverse, inverse


def norm_back(d_normed, unit, inverse, gain):
    d_unit = d_normed * gain
    return inverse * (
        d_unit
        - jnp.mean(d_unit, -1, keepdims=True)
        - unit * jnp.mean(d_unit * unit, -1, keepdims=True)
    )


def keep_factor(words, flag, selector):
    kept = words * flag
    bits = cat([(lax.shift_right_logical(kept, s) & 1).astype(F32) for s in range(BITS)], 0)
    return mm(bits.astype(BF), selector, TN) * KEEP_SCALE


def make_selector():
    line = lax.broadcasted_iota(jnp.int32, (16 * BITS, D), 0)
    channel = lax.broadcasted_iota(jnp.int32, (16 * BITS, D), 1)
    return (channel == (line & 15) * BITS + (line >> 4)).astype(F32).astype(BF)


ROOT_HALF = 0.7071067811865476
DENSITY = 0.3989422804014327


def ffn_prepare(w_up, up_bias, w_down, up3, upt3, down3, bias_t):
    for f in range(4):
        block = w_up[:, 256 * f : 256 * f + 256]
        high, low = split(block)
        up3[f] = cat([high, low, high], 1)
        high, low = split(jnp.transpose(block))
        upt3[256 * f : 256 * f + 256, :] = cat([high, low, high], 1)
        high, low = split(w_down[256 * f : 256 * f + 256, :])
        down3[256 * f : 256 * f + 256, :] = cat([high, low, high], 1)
        bias = jnp.broadcast_to(up_bias[:, 256 * f : 256 * f + 256], (256, 256))
        bias_t[256 * f : 256 * f + 256, :] = jnp.transpose(bias)


def ffn_chunk(x, up, factor, gain, shift, up3, upt3, down3, bias_t, d_up_t, d_down, d_bias, first):
    unit, inverse = norm_stats(x)
    normed = unit * gain + shift
    grad = up * factor
    nh, nl = split(normed)
    gh, gl = split(grad)
    n_lanes, g_lanes = cat([nh, nh, nl], 1), cat([gh, gh, gl], 1)
    n_rows, g_rows = cat([nh, nh, nl], 0), cat([gh, gh, gl], 0)
    dn_t = None
    for f in range(4):
        rows = slice(256 * f, 256 * f + 256)
        pre = mm(upt3[rows, :], n_lanes, NT) + bias_t[rows, :]
        d_hidden = mm(down3[rows, :], g_lanes, NT)
        cdf = 0.5 * (1.0 + lax.erf(pre * ROOT_HALF))
        density = DENSITY * jnp.exp(-0.5 * pre * pre)
        hidden = pre * cdf
        d_pre = d_hidden * (cdf + pre * density)
        hh, hl = split(hidden)
        ph, pw = split(d_pre)
        part = mm(up3[f], cat([ph, ph, pw], 0), NN)
        dn_t = part if dn_t is None else dn_t + part
        down_part = mm(cat([hh, hl, hh], 1), g_rows, NN)
        up_part = mm(cat([ph, pw, ph], 1), n_rows, NN)
        bias_part = d_pre[:, :128] + d_pre[:, 128:]
        if first is True:
            d_down[rows, :] = down_part
            d_up_t[rows, :] = up_part
            d_bias[rows, :] = bias_part
        else:
            d_down[rows, :] += down_part
            d_up_t[rows, :] += up_part
            d_bias[rows, :] += bias_part
    d_normed = jnp.transpose(dn_t)
    d_x = norm_back(d_normed, unit, inverse, gain)
    return d_x, d_normed * unit, d_normed


def fold_rows(x):
    rows = x.shape[0]
    return jnp.sum(x.reshape(rows // 8, 8, x.shape[1]), axis=0)


def head_mask(rows, head):
    lane = lax.broadcasted_iota(jnp.int32, (rows, D), 1)
    return (lane >> 5) == head


def spread_heads(x):
    zero = jnp.zeros_like(x)
    return cat([jnp.where(head_mask(64, h), x, zero) for h in range(NH)], 0)


def pick_heads(full):
    out = full[0:64]
    for h in range(1, NH):
        out = jnp.where(head_mask(64, h), full[64 * h : 64 * h + 64], out)
    return out


def group_core(q, k, v, g):
    qh, ql = split(q)
    kh, kl = split(k)
    vh, vl = split(v)
    gh, gl = split(g)
    q_high, q_low = spread_heads(qh), spread_heads(ql)
    g_high, g_low = spread_heads(gh), spread_heads(gl)
    two = mm(cat([kh, kl], 0), q_high, NT)
    scores = two[:64] + two[64:] + mm(kh, q_low, NT)
    scores = jnp.exp(scores - jnp.max(scores, axis=0, keepdims=True))
    p = scores * (1.0 / jnp.sum(scores, axis=0, keepdims=True))
    two = mm(cat([vh, vl], 0), g_high, NT)
    dp = two[:64] + two[64:] + mm(vh, g_low, NT)
    ds = p * (dp - jnp.sum(p * dp, axis=0, keepdims=True))
    ph, pw = split(p)
    sh, sw = split(ds)
    two = mm(cat([ph, pw], 0), g_high, NN)
    dv = two[:64] + two[64:] + mm(ph, g_low, NN)
    two = mm(cat([sh, sw], 0), q_high, NN)
    dk = two[:64] + two[64:] + mm(sh, q_low, NN)
    mixed = pick_heads(mm(cat([ph, pw, ph], 0), cat([vh, vh, vl], 0), TN))
    dq = pick_heads(mm(cat([sh, sw, sh], 0), cat([kh, kh, kl], 0), TN))
    return mixed, dq, dk, dv


def get(ref, part, rows):
    return cat([ref[2 * part, rows, :], ref[2 * part + 1, rows, :]], 1)


def put(ref, part, rows, x):
    ref[2 * part, rows, :] = x[:, :128]
    ref[2 * part + 1, rows, :] = x[:, 128:]

MESH = pl.DeviceIdType.MESH
MID_GROUP = 10


def remote(src, dst, send, recv, device):
    return pltpu.make_async_remote_copy(
        src_ref=src, dst_ref=dst, send_sem=send, recv_sem=recv, device_id=(device,), device_id_type=MESH
    )


def arrived(ref, sem):
    pltpu.make_async_copy(ref, ref, sem).wait()


def kernel(tokens, stored, upstream, drop_attn, drop_ffn, depth_keep, gain_one, shift_one, w_qkv, w_out,
           gain_two, shift_two, w_up, up_bias, w_down,
           result, out_gain_one, out_shift_one, out_qkv, out_out, out_gain_two, out_shift_two, out_up, out_bias, out_down,
           up3, upt3, down3, bias_t, d_bias, factor_ffn, factor_attn, through, branch,
           grid_tokens, grid_grad, d_grid, back,
           ffn_sum, ffn_half, ffn_slots, ffn_mine, ffn_all,
           att_sum, att_half, att_slots, att_mine, att_all,
           vec_two, vec_two_slots, vec_one, vec_one_slots, vec_core, vec_pair,
           qkv, mixed, d_qkv, d_mixed, unit_s, inverse_s, normed_t,
           send, recv, local):
    me = lax.axis_index("rows")
    spot, core = me // 2, me % 2
    pair = me + 1 - 2 * core
    band, lane = me // 16, me % 16
    grad_scale = float(1024 * 128) ** (-0.5)

    def same_core(k):
        return ((spot + k) % 64) * 2 + core

    barrier = pltpu.get_barrier_semaphore()

    @pl.loop(1, 64)
    def _(k):
        pl.semaphore_signal(barrier, inc=1, device_id=(same_core(k),), device_id_type=MESH)

    pl.semaphore_signal(barrier, inc=1, device_id=(pair,), device_id_type=MESH)

    ffn_prepare(w_up, up_bias, w_down, up3, upt3, down3, bias_t)
    selector = make_selector()
    zeros = jnp.zeros((2, 1024), jnp.int32)
    tile = lax.broadcasted_iota(jnp.int32, (128, 1024), 0)
    column = lax.broadcasted_iota(jnp.int32, (128, 1024), 1)
    widen = (tile == (column >> 3)).astype(F32).astype(BF)
    flags = [
        mm(jnp.broadcast_to(depth_keep[n, pl.ds(me // 8, 1), :].astype(F32), (8, 128)).astype(BF), widen, NN)[0:1].astype(jnp.int32)
        for n in range(2)
    ]
    for n, (words, factor) in enumerate(((drop_attn, factor_attn), (drop_ffn, factor_ffn))):
        kept = keep_factor(cat([words[...], zeros], 0), flags[n], selector)
        factor[...] = kept.reshape(8, 128, D)

    pl.semaphore_wait(barrier, 64)

    def token_piece(who):
        return tokens.at[:, pl.ds(pl.multiple_of(16 * who, 16), 16), :]

    def branch_piece(who):
        return branch.at[:, pl.ds(pl.multiple_of(16 * who, 16), 16), :]

    own_tokens = pltpu.make_async_copy(token_piece(band), grid_tokens.at[band], recv.at[0])
    own_tokens.start()

    @pl.loop(1, 8)
    def _(k):
        who = (band + k) % 8
        remote(token_piece(who), grid_tokens.at[band], send.at[0], recv.at[0], who * 16 + lane).start()

    ffn_sum[...] = jnp.zeros_like(ffn_sum)
    d_bias[...] = jnp.zeros_like(d_bias)
    vec_two[...] = jnp.zeros_like(vec_two)
    d_up_t, d_down = ffn_sum.at[0:1024], ffn_sum.at[1024:2048]

    def send_branch(who):
        remote(branch_piece(who), grid_grad.at[band], send.at[1], recv.at[1], who * 16 + lane).start()

    @pl.loop(0, 4)
    def _(s):
        offset = 2 - s + 3 * (s // 2) - 2 * (s // 3)
        q = (band // 2 + offset) % 4
        cols = pl.ds(pl.multiple_of(q * 32, 32), 32)
        up = upstream[:, cols, :].reshape(256, D)
        d_x, d_gain, d_shift = ffn_chunk(
            stored[:, cols, :].reshape(256, D), up, factor_ffn[:, cols, :].reshape(256, D),
            gain_two[...], shift_two[...], up3, upt3, down3, bias_t, d_up_t, d_down, d_bias, False)
        total = up + d_x
        through[:, cols, :] = total.reshape(8, 32, D)
        branch[:, cols, :] = (total * factor_attn[:, cols, :].reshape(256, D)).reshape(8, 32, D)
        vec_two[0:1, :] += jnp.sum(d_gain, axis=0, keepdims=True)
        vec_two[1:2, :] += jnp.sum(d_shift, axis=0, keepdims=True)

        @pl.when(s < 3)
        def _():
            send_branch(2 * q)
            send_branch(2 * q + 1)

        @pl.when(s == 3)
        def _():
            send_branch(band + 1 - 2 * (band % 2))
            pltpu.make_async_copy(branch_piece(band), grid_grad.at[band], recv.at[1]).start()

    for f in range(4):
        vec_two[2 + f : 3 + f, :] = jnp.sum(jnp.transpose(d_bias[256 * f : 256 * f + 256, :]), axis=0, keepdims=True)

    ffn_pair = remote(
        ffn_sum.at[pl.ds(pl.multiple_of((1 - core) * 1024, 1024), 1024)], ffn_half, send.at[2], recv.at[2], pair)
    ffn_pair.start()
    own_vec_two = pltpu.make_async_copy(vec_two, vec_two_slots.at[spot], recv.at[3])
    own_vec_two.start()

    @pl.loop(1, 64)
    def _(k):
        remote(vec_two, vec_two_slots.at[spot], send.at[3], recv.at[3], same_core(k)).start()

    scale = HD ** (-0.5)
    wh, wl = split(w_qkv[...])
    w_rows = cat([wh, wh, wl], 0)
    arrived(grid_tokens, recv.at[0])
    for c in range(4):
        rows = slice(256 * c, 256 * c + 256)
        unit, inverse = norm_stats(grid_tokens[2 * c : 2 * c + 2].reshape(256, D))
        unit_s[rows, :] = unit
        inverse_s[rows, :] = jnp.broadcast_to(inverse, (256, 128))
        normed = unit * gain_one[...] + shift_one[...]
        normed_t[:, rows] = jnp.transpose(normed)
        nh, nl = split(normed)
        out = mm(cat([nh, nl, nh], 1), w_rows, NN)
        put(qkv, 0, rows, out[:, :256] * scale)
        put(qkv, 1, rows, out[:, 256:512])
        put(qkv, 2, rows, out[:, 512:])

    ffn_pair.wait()
    ffn_half[...] += ffn_sum[pl.ds(pl.multiple_of(core * 1024, 1024), 1024), :]

    @pl.loop(1, 64)
    def _(k):
        rows = pl.ds(pl.multiple_of(((spot + k) % 64) * 16, 16), 16)
        remote(ffn_half.at[rows], ffn_slots.at[k - 1], send.at[4], recv.at[4], same_core(k)).start()

    oh, ol = split(w_out[...])
    o_lanes = cat([oh, oh, ol], 1)
    arrived(grid_grad, recv.at[1])
    for c in range(4):
        rows = slice(256 * c, 256 * c + 256)
        gh, gl = split(grid_grad[2 * c : 2 * c + 2].reshape(256, D))
        put(d_mixed, 0, rows, mm(cat([gh, gl, gh], 1), o_lanes, NT))

    def ffn_gather(k):
        rows = pl.ds(pl.multiple_of(core * 1024 + spot * 16, 16), 16)
        return ffn_all.at[rows]

    @pl.loop(0, 16)
    def _(b):
        own = pl.ds(b, 64, stride=16)
        m, dq, dk, dv = group_core(get(qkv, 0, own), get(qkv, 1, own), get(qkv, 2, own), get(d_mixed, 0, own))
        put(mixed, 0, own, m)
        put(d_qkv, 0, own, dq * scale)
        put(d_qkv, 1, own, dk)
        put(d_qkv, 2, own, dv)

        @pl.when(b == MID_GROUP)
        def _():
            arrived(ffn_slots, recv.at[4])
            mine = ffn_half[pl.ds(pl.multiple_of(spot * 16, 16), 16), :]
            ffn_mine[...] = (mine + jnp.sum(ffn_slots[...], axis=0)) * grad_scale
            pltpu.make_async_copy(ffn_mine, ffn_gather(0), recv.at[5]).start()

            @pl.loop(1, 64)
            def _(k):
                remote(ffn_mine, ffn_gather(k), send.at[5], recv.at[5], same_core(k)).start()

    w_lanes = cat([wh, wh, wl], 1)
    d_gain = jnp.zeros((8, D), F32)
    d_shift = jnp.zeros((8, D), F32)

    def back_piece(who):
        return back.at[:, pl.ds(pl.multiple_of(16 * who, 16), 16), :]

    for c in range(4):
        rows = slice(256 * c, 256 * c + 256)
        dh, dl = split(cat([d_qkv[i, rows, :] for i in range(6)], 1))
        dn = mm(cat([dh, dl, dh], 1), w_lanes, NT)
        unit = unit_s[rows, :]
        inverse = inverse_s[rows, 0:1]
        d_grid[2 * c : 2 * c + 2] = norm_back(dn, unit, inverse, gain_one[...]).reshape(2, 8, 16, D)
        d_gain += fold_rows(dn * unit)
        d_shift += fold_rows(dn)

    pltpu.make_async_copy(d_grid.at[band], back_piece(band), recv.at[6]).start()

    @pl.loop(1, 8)
    def _(k):
        who = (band + k) % 8
        remote(d_grid.at[who], back_piece(band), send.at[6], recv.at[6], who * 16 + lane).start()

    vec_one[0:1, :] = jnp.sum(d_gain, axis=0, keepdims=True)
    vec_one[1:2, :] = jnp.sum(d_shift, axis=0, keepdims=True)
    pltpu.make_async_copy(vec_one, vec_one_slots.at[spot], recv.at[7]).start()

    @pl.loop(1, 64)
    def _(k):
        remote(vec_one, vec_one_slots.at[spot], send.at[7], recv.at[7], same_core(k)).start()

    for c in range(4):
        rows = slice(256 * c, 256 * c + 256)
        dh, dl = split(cat([d_qkv[i, rows, :] for i in range(6)], 1))
        nh, nl = split(normed_t[:, rows])
        part = mm(cat([nh, nl, nh], 1), cat([dh, dh, dl], 0), NN)
        mh, ml = split(jnp.transpose(get(mixed, 0, rows)))
        gh, gl = split(grid_grad[2 * c : 2 * c + 2].reshape(256, D))
        part_o = mm(cat([mh, ml, mh], 1), cat([gh, gh, gl], 0), NN)
        for n in range(4):
            piece = part_o if n == 3 else part[:, 256 * n : 256 * n + 256]
            if c == 0:
                att_sum[256 * n : 256 * n + 256, :] = piece
            else:
                att_sum[256 * n : 256 * n + 256, :] += piece

    att_pair = remote(
        att_sum.at[pl.ds(pl.multiple_of((1 - core) * 512, 512), 512)], att_half, send.at[8], recv.at[8], pair)
    att_pair.start()

    arrived(ffn_all.at[pl.ds(pl.multiple_of(core * 1024, 1024), 1024)], recv.at[5])
    ffn_rows = ffn_all.at[pl.ds(pl.multiple_of(core * 1024, 1024), 1024)]
    ffn_swap = remote(ffn_rows, ffn_rows, send.at[9], recv.at[9], pair)
    ffn_swap.start()

    att_pair.wait()
    att_half[...] += att_sum[pl.ds(pl.multiple_of(core * 512, 512), 512), :]

    @pl.loop(1, 64)
    def _(k):
        rows = pl.ds(pl.multiple_of(((spot + k) % 64) * 8, 8), 8)
        remote(att_half.at[rows], att_slots.at[k - 1], send.at[10], recv.at[10], same_core(k)).start()

    arrived(vec_two_slots, recv.at[3])
    arrived(vec_one_slots, recv.at[7])
    vec_core[0:8, :] = jnp.sum(vec_two_slots[...], axis=0)
    vec_core[8:10, :] = jnp.sum(vec_one_slots[...], axis=0)
    vec_core[10:16, :] = jnp.zeros((6, D), F32)
    vec_swap = remote(vec_core, vec_pair, send.at[11], recv.at[11], pair)
    vec_swap.start()

    arrived(back, recv.at[6])
    result[...] = through[...] + back[...]
    vec_swap.wait()
    total = (vec_core[...] + vec_pair[...]) * grad_scale
    out_gain_two[...] = total[0:1]
    out_shift_two[...] = total[1:2]
    for f in range(4):
        out_bias[:, 256 * f : 256 * f + 256] = total[2 + f : 3 + f]
    out_gain_one[...] = total[8:9]
    out_shift_one[...] = total[9:10]

    arrived(att_slots, recv.at[10])
    mine = att_half[pl.ds(pl.multiple_of(spot * 8, 8), 8), :]
    att_mine[...] = (mine + jnp.sum(att_slots[...], axis=0)) * grad_scale
    att_spot = att_all.at[pl.ds(pl.multiple_of(core * 512 + spot * 8, 8), 8)]
    pltpu.make_async_copy(att_mine, att_spot, recv.at[12]).start()

    @pl.loop(1, 64)
    def _(k):
        remote(att_mine, att_spot, send.at[12], recv.at[12], same_core(k)).start()

    ffn_swap.wait()
    for f in range(4):
        rows = slice(256 * f, 256 * f + 256)
        out_up[:, rows] = jnp.transpose(ffn_all[rows, :])
        out_down[rows, :] = ffn_all[1024 + 256 * f : 1280 + 256 * f, :]

    att_rows = att_all.at[pl.ds(pl.multiple_of(core * 512, 512), 512)]
    arrived(att_rows, recv.at[12])
    att_swap = remote(att_rows, att_rows, send.at[13], recv.at[13], pair)
    att_swap.start()
    arrived(grid_tokens.at[0:7], send.at[0])
    arrived(grid_grad.at[0:7], send.at[1])
    arrived(vec_two_slots.at[0:63], send.at[3])
    arrived(ffn_slots, send.at[4])
    arrived(ffn_slots, send.at[5])
    arrived(d_grid.at[0:7], send.at[6])
    arrived(vec_one_slots.at[0:63], send.at[7])
    arrived(att_slots, send.at[10])
    arrived(att_slots, send.at[12])
    att_swap.wait()
    for n in range(3):
        out_qkv[:, 256 * n : 256 * n + 256] = att_all[256 * n : 256 * n + 256, :]
    out_out[...] = att_all[768:1024, :]


VM = pl.BlockSpec(memory_space=pltpu.VMEM)
HB = pl.BlockSpec(memory_space=pl.ANY)
LIMIT = 62 * 1024 * 1024


def shape(*dims):
    return jax.ShapeDtypeStruct(dims, F32)


def local(tokens, stored, upstream, drop_attn, drop_ffn, depth_keep, gain_one, shift_one, w_qkv, w_out,
          gain_two, shift_two, w_up, up_bias, w_down):
    def v(*dims):
        return pltpu.VMEM(dims, F32)

    outs = pl.pallas_call(
        kernel,
        out_shape=(shape(8, 128, D), shape(1, D), shape(1, D), shape(D, 768), shape(D, D), shape(1, D), shape(1, D),
                   shape(D, FF), shape(1, FF), shape(FF, D)),
        in_specs=[HB] + [VM] * 14,
        out_specs=(VM,) * 10,
        scratch_shapes=[
            pltpu.VMEM((4, 256, 768), BF), pltpu.VMEM((1024, 768), BF), pltpu.VMEM((1024, 768), BF),
            v(1024, 256), v(1024, 128), v(8, 128, D), v(8, 128, D), v(8, 128, D), v(8, 128, D),
            v(8, 8, 16, D), v(8, 8, 16, D), v(8, 8, 16, D), v(8, 128, D),
            v(2048, D), v(1024, D), v(63, 16, D), v(16, D), v(2048, D),
            v(1024, D), v(512, D), v(63, 8, D), v(8, D), v(1024, D),
            v(8, D), v(64, 8, D), v(2, D), v(64, 2, D), v(16, D), v(16, D),
            v(6, 1024, 128), v(2, 1024, 128), v(6, 1024, 128), v(2, 1024, 128), v(1024, 256), v(1024, 128), v(256, 1024),
            pltpu.SemaphoreType.DMA((14,)), pltpu.SemaphoreType.DMA((14,)), pltpu.SemaphoreType.DMA((1,))],
        compiler_params=pltpu.CompilerParams(vmem_limit_bytes=LIMIT, collective_id=0, has_side_effects=True),
        name="block_back",
    )(tokens.reshape(8, 128, D), stored.reshape(8, 128, D), upstream.reshape(8, 128, D), drop_attn[0], drop_ffn[0], depth_keep,
      gain_one[None], shift_one[None], w_qkv, w_out, gain_two[None], shift_two[None], w_up, up_bias[None], w_down)
    result, gain_one, shift_one, d_qkv, d_out, gain_two, shift_two, d_up, bias, d_down = outs
    return (result.reshape(1, 1024, D), gain_one[0], shift_one[0], d_qkv, d_out, gain_two[0], shift_two[0], d_up, bias[0], d_down)


def solution(mesh):
    banded = P("rows", None, None)
    return jax.shard_map(
        local,
        mesh=mesh,
        in_specs=(banded,) * 5 + (P(),) * 10,
        out_specs=(banded,) + (P(),) * 9,
        check_vma=False,
    )
```

```python
from functools import partial

import jax
import jax.numpy as jnp
from jax import lax
from jax.experimental import pallas as pl
from jax.experimental.pallas import tpu as pltpu
from jax.sharding import PartitionSpec as P

NH = 8
HD = 32
D = 256
FF = 1024
EPSILON = 1e-05
KEEP_SCALE = 8.0 / 3.0
BITS = 19
BF = jnp.bfloat16
F32 = jnp.float32

NN = (((1,), (0,)), ((), ()))
NT = (((1,), (1,)), ((), ()))
TN = (((0,), (0,)), ((), ()))


def mm(a, b, dims):
    return lax.dot_general(a, b, dims, preferred_element_type=F32)


def split(x):
    high = x.astype(BF)
    return high, (x - high.astype(F32)).astype(BF)


def cat(parts, axis):
    return jnp.concatenate(parts, axis=axis)


def norm_stats(x):
    average = jnp.mean(x, -1, keepdims=True)
    centred = x - average
    spread = jnp.mean(centred * centred, -1, keepdims=True)
    inverse = lax.rsqrt(spread + EPSILON)
    return centred * inverse, inverse


def norm_back(d_normed, unit, inverse, gain):
    d_unit = d_normed * gain
    return inverse * (
        d_unit
        - jnp.mean(d_unit, -1, keepdims=True)
        - unit * jnp.mean(d_unit * unit, -1, keepdims=True)
    )


def keep_factor(words, flag, selector):
    kept = words * flag
    bits = cat([(lax.shift_right_logical(kept, s) & 1).astype(F32) for s in range(BITS)], 0)
    return mm(bits.astype(BF), selector, TN) * KEEP_SCALE


def make_selector():
    line = lax.broadcasted_iota(jnp.int32, (16 * BITS, D), 0)
    channel = lax.broadcasted_iota(jnp.int32, (16 * BITS, D), 1)
    return (channel == (line & 15) * BITS + (line >> 4)).astype(F32).astype(BF)


ROOT_HALF = 0.7071067811865476
DENSITY = 0.3989422804014327


def ffn_prepare(w_up, up_bias, w_down, up3, upt3, down3, bias_t):
    for f in range(4):
        block = w_up[:, 256 * f : 256 * f + 256]
        high, low = split(block)
        up3[f] = cat([high, low, high], 1)
        high, low = split(jnp.transpose(block))
        upt3[256 * f : 256 * f + 256, :] = cat([high, low, high], 1)
        high, low = split(w_down[256 * f : 256 * f + 256, :])
        down3[256 * f : 256 * f + 256, :] = cat([high, low, high], 1)
        bias = jnp.broadcast_to(up_bias[:, 256 * f : 256 * f + 256], (256, 256))
        bias_t[256 * f : 256 * f + 256, :] = jnp.transpose(bias)


def ffn_chunk(x, up, factor, gain, shift, up3, upt3, down3, bias_t, d_up_t, d_down, d_bias, first):
    unit, inverse = norm_stats(x)
    normed = unit * gain + shift
    grad = up * factor
    nh, nl = split(normed)
    gh, gl = split(grad)
    n_lanes, g_lanes = cat([nh, nh, nl], 1), cat([gh, gh, gl], 1)
    n_rows, g_rows = cat([nh, nh, nl], 0), cat([gh, gh, gl], 0)
    dn_t = None
    for f in range(4):
        rows = slice(256 * f, 256 * f + 256)
        pre = mm(upt3[rows, :], n_lanes, NT) + bias_t[rows, :]
        d_hidden = mm(down3[rows, :], g_lanes, NT)
        cdf = 0.5 * (1.0 + lax.erf(pre * ROOT_HALF))
        density = DENSITY * jnp.exp(-0.5 * pre * pre)
        hidden = pre * cdf
        d_pre = d_hidden * (cdf + pre * density)
        hh, hl = split(hidden)
        ph, pw = split(d_pre)
        part = mm(up3[f], cat([ph, ph, pw], 0), NN)
        dn_t = part if dn_t is None else dn_t + part
        down_part = mm(cat([hh, hl, hh], 1), g_rows, NN)
        up_part = mm(cat([ph, pw, ph], 1), n_rows, NN)
        bias_part = d_pre[:, :128] + d_pre[:, 128:]
        if first is True:
            d_down[rows, :] = down_part
            d_up_t[rows, :] = up_part
            d_bias[rows, :] = bias_part
        else:
            d_down[rows, :] += down_part
            d_up_t[rows, :] += up_part
            d_bias[rows, :] += bias_part
    d_normed = jnp.transpose(dn_t)
    d_x = norm_back(d_normed, unit, inverse, gain)
    return d_x, d_normed * unit, d_normed


def fold_rows(x):
    rows = x.shape[0]
    return jnp.sum(x.reshape(rows // 8, 8, x.shape[1]), axis=0)


def head_mask(head):
    lane = lax.broadcasted_iota(jnp.int32, (64, 128), 1)
    return (lane >> 5) == head


def spread_heads(x):
    zero = jnp.zeros_like(x)
    return cat([jnp.where(head_mask(h), x, zero) for h in range(4)], 0)


def pick_heads(full):
    out = full[0:64]
    for h in range(1, 4):
        out = jnp.where(head_mask(h), full[64 * h : 64 * h + 64], out)
    return out


def stacked(high, low, other_high, other_low, dims):
    two = mm(cat([high, low], 0), other_high, dims)
    return two[:64] + two[64:] + mm(high, other_low, dims)


def group_forward(q, k, v):
    qh, ql = split(q)
    kh, kl = split(k)
    vh, vl = split(v)
    scores = stacked(kh, kl, spread_heads(qh), spread_heads(ql), NT)
    scores = jnp.exp(scores - jnp.max(scores, axis=0, keepdims=True))
    p = scores * (1.0 / jnp.sum(scores, axis=0, keepdims=True))
    ph, pw = split(p)
    return p, pick_heads(mm(cat([ph, pw, ph], 0), cat([vh, vh, vl], 0), TN))


def group_backward(q, k, v, g, p):
    qh, ql = split(q)
    kh, kl = split(k)
    vh, vl = split(v)
    gh, gl = split(g)
    q_high, q_low = spread_heads(qh), spread_heads(ql)
    g_high, g_low = spread_heads(gh), spread_heads(gl)
    dp = stacked(vh, vl, g_high, g_low, NT)
    ph, pw = split(p)
    dv = stacked(ph, pw, g_high, g_low, NN)
    ds = p * (dp - jnp.sum(p * dp, axis=0, keepdims=True))
    sh, sw = split(ds)
    dk = stacked(sh, sw, q_high, q_low, NN)
    dq = pick_heads(mm(cat([sh, sw, sh], 0), cat([kh, kh, kl], 0), TN))
    return dq, dk, dv


def get(ref, part, rows):
    return cat([ref[2 * part, rows, :], ref[2 * part + 1, rows, :]], 1)


def put(ref, part, rows, x):
    ref[2 * part, rows, :] = x[:, :128]
    ref[2 * part + 1, rows, :] = x[:, 128:]

MESH = pl.DeviceIdType.MESH
UNROLL_FORWARD = 2
UNROLL_BACK = 4


def remote(src, dst, send, recv, device):
    return pltpu.make_async_remote_copy(
        src_ref=src, dst_ref=dst, send_sem=send, recv_sem=recv, device_id=(device,), device_id_type=MESH
    )


def arrived(ref, sem):
    pltpu.make_async_copy(ref, ref, sem).wait()


def at_rows(ref, start, size):
    return ref.at[pl.ds(pl.multiple_of(start, 8), size)]


def kernel(tokens, stored, upstream, drop_attn, drop_ffn, depth_keep, gain_one, shift_one, w_qkv, w_out,
           gain_two, shift_two, w_up, up_bias, w_down,
           through, back, ffn_all, att_all, vec_total,
           up3, upt3, down3, bias_t, d_bias, factor_ffn, factor_attn, branch,
           grid_tokens, grid_grad, d_grid,
           ffn_sum, ffn_half, slots_a, slots_b, slots_c,
           att_sum, att_half, att_slots, att_mine,
           vec, vec_slots,
           qkv, weights, mixed, d_qkv, d_mixed, unit_s, inverse_s, normed3, grad3,
           send, recv):
    me = lax.axis_index("rows")
    spot, core = me // 2, me % 2
    pair = me + 1 - 2 * core
    band, lane = me // 16, me % 16
    x, y, z = me // 32, (me // 8) % 4, (me // 2) % 4
    grad_scale = float(1024 * 128) ** (-0.5)
    steps = {"x": (x, 32), "y": (y, 8), "z": (z, 2)}

    def same_core(k):
        return ((spot + k) % 64) * 2 + core

    def along(axis, k):
        at, stride = steps[axis]
        return me + (((at + k) % 4) - at) * stride

    barrier = pltpu.get_barrier_semaphore()

    @pl.loop(1, 64)
    def _(k):
        pl.semaphore_signal(barrier, inc=1, device_id=(same_core(k),), device_id_type=MESH)

    pl.semaphore_signal(barrier, inc=1, device_id=(pair,), device_id_type=MESH)

    ffn_prepare(w_up, up_bias, w_down, up3, upt3, down3, bias_t)
    selector = make_selector()
    zeros = jnp.zeros((2, 1024), jnp.int32)
    tile = lax.broadcasted_iota(jnp.int32, (128, 1024), 0)
    column = lax.broadcasted_iota(jnp.int32, (128, 1024), 1)
    widen = (tile == (column >> 3)).astype(F32).astype(BF)
    flags = [
        mm(jnp.broadcast_to(depth_keep[n, pl.ds(me // 8, 1), :].astype(F32), (8, 128)).astype(BF), widen, NN)[0:1].astype(jnp.int32)
        for n in range(2)
    ]
    for n, (words, factor) in enumerate(((drop_attn, factor_attn), (drop_ffn, factor_ffn))):
        kept = keep_factor(cat([words[0], zeros], 0), flags[n], selector)
        factor[...] = kept.reshape(8, 128, D)

    def piece(ref, who):
        return ref.at[:, pl.ds(pl.multiple_of(16 * who, 16), 16), :]

    ffn_sum[...] = jnp.zeros_like(ffn_sum)
    d_bias[...] = jnp.zeros_like(d_bias)
    vec[...] = jnp.zeros_like(vec)
    d_up_t, d_down = ffn_sum.at[0:1024], ffn_sum.at[1024:2048]

    def send_branch(who):
        remote(piece(branch, who), grid_grad.at[band], send.at[1], recv.at[1], who * 16 + lane).start()

    pl.semaphore_wait(barrier, 64)
    pltpu.make_async_copy(piece(tokens, band), grid_tokens.at[band], recv.at[0]).start()

    @pl.loop(1, 8)
    def _(k):
        who = (band + k) % 8
        remote(piece(tokens, who), grid_tokens.at[band], send.at[0], recv.at[0], who * 16 + lane).start()

    @pl.loop(0, 4)
    def _(s):
        offset = 2 - s + 3 * (s // 2) - 2 * (s // 3)
        q = (band // 2 + offset) % 4
        cols = pl.ds(pl.multiple_of(q * 32, 32), 32)
        up = upstream[:, cols, :].reshape(256, D)
        d_x, d_gain, d_shift = ffn_chunk(
            stored[:, cols, :].reshape(256, D), up, factor_ffn[:, cols, :].reshape(256, D),
            gain_two[...], shift_two[...], up3, upt3, down3, bias_t, d_up_t, d_down, d_bias, False)
        total = up + d_x
        through[:, cols, :] = total.reshape(8, 32, D)
        branch[:, cols, :] = (total * factor_attn[:, cols, :].reshape(256, D)).reshape(8, 32, D)
        vec[0:1, :] += jnp.sum(d_gain, axis=0, keepdims=True)
        vec[1:2, :] += jnp.sum(d_shift, axis=0, keepdims=True)

        @pl.when(s < 3)
        def _():
            send_branch(2 * q)
            send_branch(2 * q + 1)

        @pl.when(s == 3)
        def _():
            send_branch(band + 1 - 2 * (band % 2))
            pltpu.make_async_copy(piece(branch, band), grid_grad.at[band], recv.at[1]).start()

    for f in range(4):
        vec[2 + f : 3 + f, :] = jnp.sum(jnp.transpose(d_bias[256 * f : 256 * f + 256, :]), axis=0, keepdims=True)

    def vec_start(n, axis):
        at = core if axis == "core" else steps[axis][0]
        pltpu.make_async_copy(vec, vec_slots.at[n, at], recv.at[16 + n]).start()
        for k in range(1, 2 if axis == "core" else 4):
            to = pair if axis == "core" else along(axis, k)
            remote(vec, vec_slots.at[n, at], send.at[16 + n], recv.at[16 + n], to).start()

    def vec_finish(n, axis):
        if axis == "core":
            arrived(vec_slots.at[n, 0:2], recv.at[16 + n])
            arrived(vec_slots.at[n, 0], send.at[16 + n])
            return vec_slots[n, 0] + vec_slots[n, 1]
        arrived(vec_slots.at[n], recv.at[16 + n])
        arrived(vec_slots.at[n, 0:3], send.at[16 + n])
        return (vec_slots[n, 0] + vec_slots[n, 1]) + (vec_slots[n, 2] + vec_slots[n, 3])

    mine = core * 1024
    ffn_pair = remote(at_rows(ffn_sum, (1 - core) * 1024, 1024), ffn_half, send.at[2], recv.at[2], pair)
    ffn_pair.start()
    orders = (("z", "x", "y"), ("y", "z", "x"))
    sizes = (128, 32, 8)
    slots = (slots_a, slots_b, slots_c)

    def block_start(part, step):
        start = 512 * part
        for n in range(step):
            start = start + steps[orders[part][n]][0] * sizes[n]
        return start

    def ffn_scatter_start(step):
        for part in range(2):
            axis = orders[part][step]
            sem = 24 + 3 * part + step
            for k in range(1, 4):
                to = (steps[axis][0] + k) % 4
                rows = at_rows(ffn_half, block_start(part, step) + to * sizes[step], sizes[step])
                remote(rows, slots[step].at[part, k - 1], send.at[sem], recv.at[sem], along(axis, k)).start()

    def ffn_scatter_finish(step):
        for part in range(2):
            arrived(slots[step].at[part], recv.at[24 + 3 * part + step])
            rows = pl.ds(pl.multiple_of(block_start(part, step + 1), 8), sizes[step])
            total = ffn_half[rows, :] + slots[step][part, 0] + slots[step][part, 1] + slots[step][part, 2]
            if step < 2:
                ffn_half[rows, :] = total
            else:
                ffn_all[pl.ds(pl.multiple_of(mine + block_start(part, 3), 8), 8), :] = total * grad_scale

    def ffn_gather_start(step):
        for part in range(2):
            sem = 30 + 3 * part + step
            rows = at_rows(ffn_all, mine + block_start(part, step + 1), sizes[step])
            for k in range(1, 4):
                remote(rows, rows, send.at[sem], recv.at[sem], along(orders[part][step], k)).start()

    def ffn_gather_finish(step):
        for part in range(2):
            arrived(slots[step].at[part], recv.at[30 + 3 * part + step])

    scale = HD ** (-0.5)
    wh, wl = split(w_qkv[...])
    w_rows = cat([wh, wh, wl], 0)
    arrived(grid_tokens, recv.at[0])
    for c in range(4):
        rows = slice(256 * c, 256 * c + 256)
        unit, inverse = norm_stats(grid_tokens[2 * c : 2 * c + 2].reshape(256, D))
        unit_s[rows, :] = unit
        inverse_s[rows, :] = jnp.broadcast_to(inverse, (256, 128))
        normed = unit * gain_one[...] + shift_one[...]
        nh, nl = split(jnp.transpose(normed))
        normed3[c] = cat([nh, nl, nh], 1)
        nh, nl = split(normed)
        out = mm(cat([nh, nl, nh], 1), w_rows, NN)
        put(qkv, 0, rows, out[:, :256] * scale)
        put(qkv, 1, rows, out[:, 256:512])
        put(qkv, 2, rows, out[:, 512:])

    ffn_pair.wait()
    ffn_half[...] += ffn_sum[pl.ds(pl.multiple_of(mine, 8), 1024), :]
    ffn_scatter_start(0)

    @pl.loop(0, 16 // UNROLL_FORWARD)
    def _(b):
        for n in range(UNROLL_FORWARD):
            at = b * UNROLL_FORWARD + n
            own = pl.ds(at, 64, stride=16)
            for h in range(2):
                p, m = group_forward(qkv[h, own, :], qkv[2 + h, own, :], qkv[4 + h, own, :])
                weights[h, at] = p
                mixed[h, own, :] = m

    oh, ol = split(w_out[...])
    o_lanes = cat([oh, oh, ol], 1)
    arrived(grid_grad, recv.at[1])
    for c in range(4):
        rows = slice(256 * c, 256 * c + 256)
        gh, gl = split(grid_grad[2 * c : 2 * c + 2].reshape(256, D))
        grad3[c] = cat([gh, gh, gl], 0)
        put(d_mixed, 0, rows, mm(cat([gh, gl, gh], 1), o_lanes, NT))

    def groups_back(h, b):
        for n in range(UNROLL_BACK):
            at = b * UNROLL_BACK + n
            own = pl.ds(at, 64, stride=16)
            dq, dk, dv = group_backward(
                qkv[h, own, :], qkv[2 + h, own, :], qkv[4 + h, own, :], d_mixed[h, own, :], weights[h, at])
            d_qkv[h, own, :] = dq * scale
            d_qkv[2 + h, own, :] = dk
            d_qkv[4 + h, own, :] = dv

    def weight_grads(h):
        for c in range(4):
            rows = slice(256 * c, 256 * c + 256)
            dh, dl = split(cat([d_qkv[2 * i + h, rows, :] for i in range(3)], 1))
            part = mm(normed3[c], cat([dh, dh, dl], 0), NN)
            mh, ml = split(jnp.transpose(mixed[h, rows, :]))
            part_o = mm(cat([mh, ml, mh], 1), grad3[c], NN)
            blocks = [part[:, 0:128], part[:, 128:256], part[:, 256:384], cat([part_o[:, :128], part_o[:, 128:]], 0)]
            for n, block in enumerate(blocks):
                if c == 0:
                    att_sum[h, 256 * n : 256 * n + 256, :] = block
                else:
                    att_sum[h, 256 * n : 256 * n + 256, :] += block

    def att_pair_copy(h):
        return remote(at_rows(att_sum.at[h], (1 - core) * 512, 512), att_half.at[h], send.at[9 + h], recv.at[9 + h], pair)

    def att_scatter_start(h):
        att_pair_copy(h).wait()
        att_half[h] += att_sum[h, pl.ds(pl.multiple_of(core * 512, 8), 512), :]

        @pl.loop(1, 64)
        def _(k):
            rows = at_rows(att_half.at[h], ((spot + k) % 64) * 8, 8)
            remote(rows, att_slots.at[h, k - 1], send.at[11 + h], recv.at[11 + h], same_core(k)).start()

    def att_gather_start(h):
        arrived(att_slots.at[h], recv.at[11 + h])
        own = att_half[h, pl.ds(pl.multiple_of(spot * 8, 8), 8), :]
        att_mine[h] = (own + jnp.sum(att_slots[h], axis=0)) * grad_scale
        rows = at_rows(att_all.at[h], core * 512 + spot * 8, 8)
        pltpu.make_async_copy(att_mine.at[h], rows, recv.at[13 + h]).start()

        @pl.loop(1, 64)
        def _(k):
            remote(att_mine.at[h], rows, send.at[13 + h], recv.at[13 + h], same_core(k)).start()

    def att_swap_copy(h):
        rows = at_rows(att_all.at[h], core * 512, 512)
        return remote(rows, rows, send.at[22 + h], recv.at[22 + h], pair)

    def groups_range(h, first, count):
        @pl.loop(first // UNROLL_BACK, (first + count) // UNROLL_BACK)
        def _(b):
            groups_back(h, b)

    w_lanes = cat([wh, wh, wl], 1)

    def token_grads(g):
        cols = slice(8 * g, 8 * g + 8)
        d_gain = jnp.zeros((8, D), F32)
        d_shift = jnp.zeros((8, D), F32)
        for c in range(2):
            rows = slice(512 * c, 512 * c + 512)

            def part(block):
                return block.reshape(32, 16, -1)[:, cols].reshape(256, -1)

            dh, dl = split(cat([part(d_qkv[i, rows, :]) for i in range(6)], 1))
            dn = mm(cat([dh, dl, dh], 1), w_lanes, NT)
            unit = part(unit_s[rows, :])
            inverse = part(inverse_s[rows, :])[:, 0:1]
            d_x = norm_back(dn, unit, inverse, gain_one[...])
            d_grid[g, 4 * c : 4 * c + 4] = d_x.reshape(4, 8, 8, D)
            d_gain += fold_rows(dn * unit)
            d_shift += fold_rows(dn)

        def home(who):
            return back.at[:, pl.ds(pl.multiple_of(16 * who + 8 * g, 8), 8), :]

        sem = (15, 3)[g]
        pltpu.make_async_copy(d_grid.at[g, band], home(band), recv.at[sem]).start()

        @pl.loop(1, 8)
        def _(k):
            who = (band + k) % 8
            remote(d_grid.at[g, who], home(band), send.at[sem], recv.at[sem], who * 16 + lane).start()

        return d_gain, d_shift

    groups_range(0, 0, 16)
    ffn_scatter_finish(0)
    ffn_scatter_start(1)
    weight_grads(0)
    att_pair_copy(0).start()
    groups_range(1, 0, 8)
    ffn_scatter_finish(1)
    ffn_scatter_start(2)
    att_scatter_start(0)
    gain_0, shift_0 = token_grads(0)
    vec[6:7, :] = jnp.sum(gain_0, axis=0, keepdims=True)
    vec[7:8, :] = jnp.sum(shift_0, axis=0, keepdims=True)
    groups_range(1, 8, 8)
    ffn_scatter_finish(2)
    ffn_gather_start(2)
    gain_1, shift_1 = token_grads(1)
    vec[6:7, :] += jnp.sum(gain_1, axis=0, keepdims=True)
    vec[7:8, :] += jnp.sum(shift_1, axis=0, keepdims=True)
    vec_start(0, "core")
    ffn_gather_finish(2)
    ffn_gather_start(1)
    att_gather_start(0)
    weight_grads(1)
    att_pair_copy(1).start()
    ffn_gather_finish(1)
    ffn_gather_start(0)
    vec[...] = vec_finish(0, "core")
    vec_start(1, "x")
    att_scatter_start(1)
    arrived(at_rows(att_all.at[0], core * 512, 512), recv.at[13])
    att_swap_copy(0).start()
    vec[...] = vec_finish(1, "x")
    vec_start(2, "y")
    att_gather_start(1)
    vec[...] = vec_finish(2, "y")
    vec_start(3, "z")
    ffn_gather_finish(0)
    ffn_rows = at_rows(ffn_all, mine, 1024)
    ffn_swap = remote(ffn_rows, ffn_rows, send.at[20], recv.at[20], pair)
    ffn_swap.start()
    vec_total[...] = vec_finish(3, "z") * grad_scale
    arrived(at_rows(att_all.at[1], core * 512, 512), recv.at[14])
    att_swap_copy(1).start()
    arrived(d_grid.at[0], recv.at[15])
    arrived(d_grid.at[1], recv.at[3])
    arrived(grid_tokens.at[0:7], send.at[0])
    arrived(grid_grad.at[0:7], send.at[1])
    for part in range(2):
        for step in range(3):
            arrived(slots[step].at[part], send.at[24 + 3 * part + step])
            arrived(slots[step].at[part], send.at[30 + 3 * part + step])
    for h in range(2):
        arrived(att_slots.at[h], send.at[11 + h])
        arrived(att_slots.at[h], send.at[13 + h])
    arrived(d_grid.at[0, 0:7], send.at[15])
    arrived(d_grid.at[1, 0:7], send.at[3])
    ffn_swap.wait()
    att_swap_copy(0).wait()
    att_swap_copy(1).wait()


def finish_kernel(through, back, ffn_all, att_all, vec,
                  result, out_gain_one, out_shift_one, out_qkv, out_out, out_gain_two, out_shift_two, out_up, out_bias, out_down):
    result[...] = through[...] + back[...]
    out_gain_two[...] = vec[0:1, :]
    out_shift_two[...] = vec[1:2, :]
    out_gain_one[...] = vec[6:7, :]
    out_shift_one[...] = vec[7:8, :]
    for f in range(4):
        cols = slice(256 * f, 256 * f + 256)
        out_bias[:, cols] = vec[2 + f : 3 + f, :]
        out_up[:, cols] = jnp.transpose(ffn_all[cols, :])
        out_down[cols, :] = ffn_all[1024 + 256 * f : 1280 + 256 * f, :]
    for h in range(2):
        for n in range(3):
            out_qkv[:, 256 * n + 128 * h : 256 * n + 128 * h + 128] = att_all[h, 256 * n : 256 * n + 256, :]
        for n in range(2):
            out_out[128 * h : 128 * h + 128, 128 * n : 128 * n + 128] = att_all[h, 768 + 128 * n : 896 + 128 * n, :]


VM = pl.BlockSpec(memory_space=pltpu.VMEM)
HB = pl.BlockSpec(memory_space=pl.ANY)
LIMIT = 62 * 1024 * 1024


def shape(*dims):
    return jax.ShapeDtypeStruct(dims, F32)


def local(tokens, stored, upstream, drop_attn, drop_ffn, depth_keep, gain_one, shift_one, w_qkv, w_out,
          gain_two, shift_two, w_up, up_bias, w_down):
    def v(*dims):
        return pltpu.VMEM(dims, F32)

    def b(*dims):
        return pltpu.VMEM(dims, BF)

    parts = pl.pallas_call(
        kernel,
        out_shape=(shape(8, 128, D), shape(8, 128, D), shape(2048, D), shape(2, 1024, 128), shape(8, D)),
        in_specs=[HB] + [VM] * 14,
        out_specs=(VM,) * 5,
        scratch_shapes=[
            b(4, 256, 768), b(1024, 768), b(1024, 768),
            v(1024, 256), v(1024, 128), v(8, 128, D), v(8, 128, D), v(8, 128, D),
            v(8, 8, 16, D), v(8, 8, 16, D), v(2, 8, 8, 8, D),
            v(2048, D), v(1024, D), v(2, 3, 128, D), v(2, 3, 32, D), v(2, 3, 8, D),
            v(2, 1024, 128), v(2, 512, 128), v(2, 63, 8, 128), v(2, 8, 128),
            v(8, D), v(4, 4, 8, D),
            v(6, 1024, 128), v(2, 16, 64, 256), v(2, 1024, 128), v(6, 1024, 128), v(2, 1024, 128),
            v(1024, 256), v(1024, 128), b(4, 256, 768), b(4, 768, 256),
            pltpu.SemaphoreType.DMA((36,)), pltpu.SemaphoreType.DMA((36,))],
        compiler_params=pltpu.CompilerParams(vmem_limit_bytes=LIMIT, collective_id=0, has_side_effects=True),
        name="block_back",
    )(tokens.reshape(8, 128, D), stored.reshape(8, 128, D), upstream.reshape(8, 128, D), drop_attn, drop_ffn, depth_keep,
      gain_one[None], shift_one[None], w_qkv, w_out, gain_two[None], shift_two[None], w_up, up_bias[None], w_down)
    outs = pl.pallas_call(
        finish_kernel,
        out_shape=(shape(8, 128, D), shape(1, D), shape(1, D), shape(D, 768), shape(D, D), shape(1, D), shape(1, D),
                   shape(D, FF), shape(1, FF), shape(FF, D)),
        in_specs=[VM] * 5,
        out_specs=(VM,) * 10,
        compiler_params=pltpu.CompilerParams(vmem_limit_bytes=LIMIT),
        name="finish",
    )(*parts)
    result, gain_one, shift_one, d_qkv, d_out, gain_two, shift_two, d_up, bias, d_down = outs
    return (result.reshape(1, 1024, D), gain_one[0], shift_one[0], d_qkv, d_out, gain_two[0], shift_two[0], d_up, bias[0], d_down)


def solution(mesh):
    banded = P("rows", None, None)
    return jax.shard_map(
        local,
        mesh=mesh,
        in_specs=(banded,) * 5 + (P(),) * 10,
        out_specs=(banded,) + (P(),) * 9,
        check_vma=False,
    )
```

```python
from functools import partial

import jax
import jax.numpy as jnp
from jax import lax
from jax.experimental import pallas as pl
from jax.experimental.pallas import tpu as pltpu
from jax.sharding import PartitionSpec as P

NH = 8
HD = 32
D = 256
FF = 1024
EPSILON = 1e-05
KEEP_SCALE = 8.0 / 3.0
BITS = 19
BF = jnp.bfloat16
F32 = jnp.float32

NN = (((1,), (0,)), ((), ()))
NT = (((1,), (1,)), ((), ()))
TN = (((0,), (0,)), ((), ()))


def mm(a, b, dims):
    return lax.dot_general(a, b, dims, preferred_element_type=F32)


def split(x):
    high = x.astype(BF)
    return high, (x - high.astype(F32)).astype(BF)


def cat(parts, axis):
    return jnp.concatenate(parts, axis=axis)


def norm_stats(x):
    average = jnp.mean(x, -1, keepdims=True)
    centred = x - average
    spread = jnp.mean(centred * centred, -1, keepdims=True)
    inverse = lax.rsqrt(spread + EPSILON)
    return centred * inverse, inverse


def norm_back(d_normed, unit, inverse, gain):
    d_unit = d_normed * gain
    return inverse * (
        d_unit
        - jnp.mean(d_unit, -1, keepdims=True)
        - unit * jnp.mean(d_unit * unit, -1, keepdims=True)
    )


def keep_factor(words, flag, selector):
    kept = words * flag
    bits = cat([(lax.shift_right_logical(kept, s) & 1).astype(F32) for s in range(BITS)], 0)
    return mm(bits.astype(BF), selector, TN) * KEEP_SCALE


def make_selector():
    line = lax.broadcasted_iota(jnp.int32, (16 * BITS, D), 0)
    channel = lax.broadcasted_iota(jnp.int32, (16 * BITS, D), 1)
    return (channel == (line & 15) * BITS + (line >> 4)).astype(F32).astype(BF)


ROOT_HALF = 0.7071067811865476
DENSITY = 0.3989422804014327


def ffn_prepare(w_up, up_bias, w_down, up3, upt3, down3, bias_t):
    for f in range(4):
        block = w_up[:, 256 * f : 256 * f + 256]
        high, low = split(block)
        up3[f] = cat([high, low, high], 1)
        high, low = split(jnp.transpose(block))
        upt3[256 * f : 256 * f + 256, :] = cat([high, low, high], 1)
        high, low = split(w_down[256 * f : 256 * f + 256, :])
        down3[256 * f : 256 * f + 256, :] = cat([high, low, high], 1)
        bias = jnp.broadcast_to(up_bias[:, 256 * f : 256 * f + 256], (256, 256))
        bias_t[256 * f : 256 * f + 256, :] = jnp.transpose(bias)


def ffn_chunk(x, up, factor, gain, shift, up3, upt3, down3, bias_t, d_up_t, d_down, d_bias, first):
    unit, inverse = norm_stats(x)
    normed = unit * gain + shift
    grad = up * factor
    nh, nl = split(normed)
    gh, gl = split(grad)
    n_lanes, g_lanes = cat([nh, nh, nl], 1), cat([gh, gh, gl], 1)
    n_rows, g_rows = cat([nh, nh, nl], 0), cat([gh, gh, gl], 0)
    dn_t = None
    for f in range(4):
        rows = slice(256 * f, 256 * f + 256)
        pre = mm(upt3[rows, :], n_lanes, NT) + bias_t[rows, :]
        d_hidden = mm(down3[rows, :], g_lanes, NT)
        cdf = 0.5 * (1.0 + lax.erf(pre * ROOT_HALF))
        density = DENSITY * jnp.exp(-0.5 * pre * pre)
        hidden = pre * cdf
        d_pre = d_hidden * (cdf + pre * density)
        hh, hl = split(hidden)
        ph, pw = split(d_pre)
        part = mm(up3[f], cat([ph, ph, pw], 0), NN)
        dn_t = part if dn_t is None else dn_t + part
        down_part = mm(cat([hh, hl, hh], 1), g_rows, NN)
        up_part = mm(cat([ph, pw, ph], 1), n_rows, NN)
        bias_part = d_pre[:, :128] + d_pre[:, 128:]
        if first is True:
            d_down[rows, :] = down_part
            d_up_t[rows, :] = up_part
            d_bias[rows, :] = bias_part
        else:
            d_down[rows, :] += down_part
            d_up_t[rows, :] += up_part
            d_bias[rows, :] += bias_part
    d_normed = jnp.transpose(dn_t)
    d_x = norm_back(d_normed, unit, inverse, gain)
    return d_x, d_normed * unit, d_normed


def fold_rows(x):
    rows = x.shape[0]
    return jnp.sum(x.reshape(rows // 8, 8, x.shape[1]), axis=0)


def head_mask(head):
    lane = lax.broadcasted_iota(jnp.int32, (64, 128), 1)
    return (lane >> 5) == head


def spread_heads(x):
    zero = jnp.zeros_like(x)
    return cat([jnp.where(head_mask(h), x, zero) for h in range(4)], 0)


def pick_heads(full):
    out = full[0:64]
    for h in range(1, 4):
        out = jnp.where(head_mask(h), full[64 * h : 64 * h + 64], out)
    return out


def stacked(high, low, other_high, other_low, dims):
    two = mm(cat([high, low], 0), other_high, dims)
    return two[:64] + two[64:] + mm(high, other_low, dims)


def group_forward(q, k, v):
    qh, ql = split(q)
    kh, kl = split(k)
    vh, vl = split(v)
    scores = stacked(kh, kl, spread_heads(qh), spread_heads(ql), NT)
    scores = jnp.exp(scores - jnp.max(scores, axis=0, keepdims=True))
    p = scores * (1.0 / jnp.sum(scores, axis=0, keepdims=True))
    ph, pw = split(p)
    return p, pick_heads(mm(cat([ph, pw, ph], 0), cat([vh, vh, vl], 0), TN))


def group_backward(q, k, v, g, p):
    qh, ql = split(q)
    kh, kl = split(k)
    vh, vl = split(v)
    gh, gl = split(g)
    q_high, q_low = spread_heads(qh), spread_heads(ql)
    g_high, g_low = spread_heads(gh), spread_heads(gl)
    dp = stacked(vh, vl, g_high, g_low, NT)
    ph, pw = split(p)
    dv = stacked(ph, pw, g_high, g_low, NN)
    ds = p * (dp - jnp.sum(p * dp, axis=0, keepdims=True))
    sh, sw = split(ds)
    dk = stacked(sh, sw, q_high, q_low, NN)
    dq = pick_heads(mm(cat([sh, sw, sh], 0), cat([kh, kh, kl], 0), TN))
    return dq, dk, dv


def get(ref, part, rows):
    return cat([ref[2 * part, rows, :], ref[2 * part + 1, rows, :]], 1)


def put(ref, part, rows, x):
    ref[2 * part, rows, :] = x[:, :128]
    ref[2 * part + 1, rows, :] = x[:, 128:]

MESH = pl.DeviceIdType.MESH
UNROLL_FORWARD = 4
UNROLL_BACK = 2
ATT_DIRECT = (False, True)
FFN_ORDERS = (("z", "x", "y"), ("z", "y", "x"))
ATT_ORDERS = (("z", "x", "y"), ("z", "y", "x"))


def remote(src, dst, send, recv, device):
    return pltpu.make_async_remote_copy(
        src_ref=src, dst_ref=dst, send_sem=send, recv_sem=recv, device_id=(device,), device_id_type=MESH
    )


def arrived(ref, sem):
    pltpu.make_async_copy(ref, ref, sem).wait()


def at_rows(ref, start, size):
    return ref.at[pl.ds(pl.multiple_of(start, 8), size)]


def kernel(tokens, stored, upstream, drop_attn, drop_ffn, depth_keep, gain_one, shift_one, w_qkv, w_out,
           gain_two, shift_two, w_up, up_bias, w_down,
           through, back, ffn_all, att_all, vec_total,
           up3, upt3, down3, bias_t, d_bias, factor_ffn, factor_attn, branch,
           grid_tokens, grid_grad, d_grid,
           ffn_sum, ffn_half, slots_a, slots_b, slots_c, slots_d, slots_e, slots_f,
           att_sum, att_half, att_slots, att_mine,
           vec, vec_slots,
           qkv, weights, mixed, d_qkv, d_mixed, unit_s, inverse_s, normed3, grad3,
           send, recv):
    me = lax.axis_index("rows")
    spot, core = me // 2, me % 2
    pair = me + 1 - 2 * core
    band, lane = me // 16, me % 16
    x, y, z = me // 32, (me // 8) % 4, (me // 2) % 4
    grad_scale = float(1024 * 128) ** (-0.5)
    steps = {"x": (x, 32), "y": (y, 8), "z": (z, 2)}

    way = 1

    def other_spot(k):
        return (spot + way * k + 64) % 64

    def other_band(k):
        return (band + way * k + 8) % 8

    def same_core(k):
        return other_spot(k) * 2 + core

    def along(axis, k):
        at, stride = steps[axis]
        return me + (((at + k) % 4) - at) * stride

    barrier = pltpu.get_barrier_semaphore()

    @pl.loop(1, 64)
    def _(k):
        pl.semaphore_signal(barrier, inc=1, device_id=(same_core(k),), device_id_type=MESH)

    pl.semaphore_signal(barrier, inc=1, device_id=(pair,), device_id_type=MESH)

    ffn_prepare(w_up, up_bias, w_down, up3, upt3, down3, bias_t)
    selector = make_selector()
    zeros = jnp.zeros((2, 1024), jnp.int32)
    tile = lax.broadcasted_iota(jnp.int32, (128, 1024), 0)
    column = lax.broadcasted_iota(jnp.int32, (128, 1024), 1)
    widen = (tile == (column >> 3)).astype(F32).astype(BF)
    flags = [
        mm(jnp.broadcast_to(depth_keep[n, pl.ds(me // 8, 1), :].astype(F32), (8, 128)).astype(BF), widen, NN)[0:1].astype(jnp.int32)
        for n in range(2)
    ]
    for which, (words, factor) in enumerate(((drop_attn, factor_attn), (drop_ffn, factor_ffn))):
        kept = keep_factor(cat([words[n] for n in range(14)] + [zeros], 0), flags[which], selector)
        factor[...] = kept.reshape(8, 128, D)

    def piece(ref, who):
        return ref.at[:, pl.ds(pl.multiple_of(16 * who, 16), 16), :]

    ffn_sum[...] = jnp.zeros_like(ffn_sum)
    d_bias[...] = jnp.zeros_like(d_bias)
    vec[...] = jnp.zeros_like(vec)
    d_up_t, d_down = ffn_sum.at[0:1024], ffn_sum.at[1024:2048]

    def send_branch(who):
        remote(piece(branch, who), grid_grad.at[band], send.at[1], recv.at[1], who * 16 + lane).start()

    @pl.loop(0, 4)
    def _(s):
        offset = 2 - s + 3 * (s // 2) - 2 * (s // 3)
        q = (band // 2 + offset) % 4
        cols = pl.ds(pl.multiple_of(q * 32, 32), 32)
        up = upstream[:, cols, :].reshape(256, D)
        d_x, d_gain, d_shift = ffn_chunk(
            stored[:, cols, :].reshape(256, D), up, factor_ffn[:, cols, :].reshape(256, D),
            gain_two[...], shift_two[...], up3, upt3, down3, bias_t, d_up_t, d_down, d_bias, False)
        total = up + d_x
        through[:, cols, :] = total.reshape(8, 32, D)
        branch[:, cols, :] = (total * factor_attn[:, cols, :].reshape(256, D)).reshape(8, 32, D)
        vec[0:1, :] += jnp.sum(d_gain, axis=0, keepdims=True)
        vec[1:2, :] += jnp.sum(d_shift, axis=0, keepdims=True)

        @pl.when(s == 0)
        def _():
            pl.semaphore_wait(barrier, 64)
            pltpu.make_async_copy(piece(tokens, band), grid_tokens.at[band], recv.at[0]).start()

            @pl.loop(1, 8)
            def _(k):
                who = other_band(k)
                remote(piece(tokens, who), grid_tokens.at[band], send.at[0], recv.at[0], who * 16 + lane).start()

        @pl.when(s < 3)
        def _():
            send_branch(2 * q)
            send_branch(2 * q + 1)

        @pl.when(s == 3)
        def _():
            send_branch(band + 1 - 2 * (band % 2))
            pltpu.make_async_copy(piece(branch, band), grid_grad.at[band], recv.at[1]).start()

    for f in range(4):
        vec[2 + f : 3 + f, :] = jnp.sum(jnp.transpose(d_bias[256 * f : 256 * f + 256, :]), axis=0, keepdims=True)

    def vec_start(n, axis):
        at = core if axis == "core" else steps[axis][0]
        pltpu.make_async_copy(vec, vec_slots.at[n, at], recv.at[16 + n]).start()
        for k in range(1, 2 if axis == "core" else 4):
            to = pair if axis == "core" else along(axis, k)
            remote(vec, vec_slots.at[n, at], send.at[16 + n], recv.at[16 + n], to).start()

    def vec_finish(n, axis):
        if axis == "core":
            arrived(vec_slots.at[n, 0:2], recv.at[16 + n])
            arrived(vec_slots.at[n, 0], send.at[16 + n])
            return vec_slots[n, 0] + vec_slots[n, 1]
        arrived(vec_slots.at[n], recv.at[16 + n])
        arrived(vec_slots.at[n, 0:3], send.at[16 + n])
        return (vec_slots[n, 0] + vec_slots[n, 1]) + (vec_slots[n, 2] + vec_slots[n, 3])

    mine = core * 1024
    ffn_pair = remote(at_rows(ffn_sum, (1 - core) * 1024, 1024), ffn_half, send.at[2], recv.at[2], pair)
    ffn_pair.start()
    class AxisSum:
        def __init__(self, half, total, base, total_base, order, sizes, slots, sem):
            self.half, self.total, self.base, self.total_base = half, total, base, total_base
            self.order, self.sizes, self.slots, self.sem = order, sizes, slots, sem

        def block(self, step):
            start = 0
            for n in range(step):
                start = start + steps[self.order[n]][0] * self.sizes[n]
            return start

        def scatter_start(self, step):
            axis, sem = self.order[step], self.sem + step
            for k in range(1, 4):
                to = (steps[axis][0] + k) % 4
                rows = at_rows(self.half, self.base + self.block(step) + to * self.sizes[step], self.sizes[step])
                remote(rows, self.slots[step].at[k - 1], send.at[sem], recv.at[sem], along(axis, k)).start()

        def scatter_finish(self, step):
            slots = self.slots[step]
            arrived(slots, recv.at[self.sem + step])
            rows = pl.ds(pl.multiple_of(self.base + self.block(step + 1), 8), self.sizes[step])
            summed = self.half[rows, :] + slots[0] + slots[1] + slots[2]
            if step < 2:
                self.half[rows, :] = summed
            else:
                rows = pl.ds(pl.multiple_of(self.total_base + self.block(3), 8), self.sizes[2])
                self.total[rows, :] = summed * grad_scale

        def gather_start(self, step):
            sem = self.sem + 3 + step
            rows = at_rows(self.total, self.total_base + self.block(step + 1), self.sizes[step])
            for k in range(1, 4):
                remote(rows, rows, send.at[sem], recv.at[sem], along(self.order[step], k)).start()

        def gather_finish(self, step):
            arrived(self.slots[step], recv.at[self.sem + 3 + step])

        def drain(self):
            for step in range(3):
                arrived(self.slots[step], send.at[self.sem + step])
                arrived(self.slots[step], send.at[self.sem + 3 + step])

    ffn_sums = [
        AxisSum(ffn_half, ffn_all, 512 * part, mine + 512 * part, FFN_ORDERS[part], (128, 32, 8),
                [slots_a.at[part], slots_b.at[part], slots_c.at[part]], 24 + 6 * part)
        for part in range(2)
    ]
    att_sums = [
        AxisSum(att_half.at[h], att_all.at[h], 0, core * 512, ATT_ORDERS[h], (128, 32, 8),
                [slots_d.at[h], slots_e.at[h], slots_f.at[h]], 36 + 6 * h)
        for h in range(2)
    ]

    def ffn_scatter_start(step):
        for part in ffn_sums:
            part.scatter_start(step)

    def ffn_scatter_finish(step):
        for part in ffn_sums:
            part.scatter_finish(step)

    def ffn_gather_start(step):
        for part in ffn_sums:
            part.gather_start(step)

    def ffn_gather_finish(step):
        for part in ffn_sums:
            part.gather_finish(step)

    scale = HD ** (-0.5)
    wh, wl = split(w_qkv[...])
    w_rows = cat([wh, wh, wl], 0)
    arrived(grid_tokens, recv.at[0])
    for c in range(4):
        rows = slice(256 * c, 256 * c + 256)
        unit, inverse = norm_stats(grid_tokens[2 * c : 2 * c + 2].reshape(256, D))
        unit_s[rows, :] = unit
        inverse_s[rows, :] = jnp.broadcast_to(inverse, (256, 128))
        normed = unit * gain_one[...] + shift_one[...]
        nh, nl = split(jnp.transpose(normed))
        normed3[c] = cat([nh, nl, nh], 1)
        nh, nl = split(normed)
        out = mm(cat([nh, nl, nh], 1), w_rows, NN)
        put(qkv, 0, rows, out[:, :256] * scale)
        put(qkv, 1, rows, out[:, 256:512])
        put(qkv, 2, rows, out[:, 512:])

    ffn_pair.wait()
    ffn_half[...] += ffn_sum[pl.ds(pl.multiple_of(mine, 8), 1024), :]
    ffn_scatter_start(0)

    @pl.loop(0, 16 // UNROLL_FORWARD)
    def _(b):
        for n in range(UNROLL_FORWARD):
            at = b * UNROLL_FORWARD + n
            own = pl.ds(at, 64, stride=16)
            for h in range(2):
                p, m = group_forward(qkv[h, own, :], qkv[2 + h, own, :], qkv[4 + h, own, :])
                weights[h, at] = p
                mixed[h, own, :] = m

    oh, ol = split(w_out[...])
    o_lanes = cat([oh, oh, ol], 1)
    arrived(grid_grad, recv.at[1])
    for c in range(4):
        rows = slice(256 * c, 256 * c + 256)
        gh, gl = split(grid_grad[2 * c : 2 * c + 2].reshape(256, D))
        grad3[c] = cat([gh, gh, gl], 0)
        put(d_mixed, 0, rows, mm(cat([gh, gl, gh], 1), o_lanes, NT))

    def groups_back(h, b):
        for n in range(UNROLL_BACK):
            at = b * UNROLL_BACK + n
            own = pl.ds(at, 64, stride=16)
            dq, dk, dv = group_backward(
                qkv[h, own, :], qkv[2 + h, own, :], qkv[4 + h, own, :], d_mixed[h, own, :], weights[h, at])
            d_qkv[h, own, :] = dq * scale
            d_qkv[2 + h, own, :] = dk
            d_qkv[4 + h, own, :] = dv

    def weight_grads(h):
        for c in range(4):
            rows = slice(256 * c, 256 * c + 256)
            dh, dl = split(cat([d_qkv[2 * i + h, rows, :] for i in range(3)], 1))
            part = mm(normed3[c], cat([dh, dh, dl], 0), NN)
            mh, ml = split(jnp.transpose(mixed[h, rows, :]))
            part_o = mm(cat([mh, ml, mh], 1), grad3[c], NN)
            blocks = [part[:, 0:128], part[:, 128:256], part[:, 256:384], cat([part_o[:, :128], part_o[:, 128:]], 0)]
            for n, block in enumerate(blocks):
                if c == 0:
                    att_sum[h, 256 * n : 256 * n + 256, :] = block
                else:
                    att_sum[h, 256 * n : 256 * n + 256, :] += block

    def att_pair_copy(h):
        return remote(at_rows(att_sum.at[h], (1 - core) * 512, 512), att_half.at[h], send.at[9 + h], recv.at[9 + h], pair)

    def att_scatter_start(h):
        att_pair_copy(h).wait()
        att_half[h] += att_sum[h, pl.ds(pl.multiple_of(core * 512, 8), 512), :]
        if not ATT_DIRECT[h]:
            att_sums[h].scatter_start(0)
            return

        @pl.loop(1, 64)
        def _(k):
            rows = at_rows(att_half.at[h], other_spot(k) * 8, 8)
            remote(rows, att_slots.at[h, k - 1], send.at[11 + h], recv.at[11 + h], same_core(k)).start()

    def att_gather_start(h):
        arrived(att_slots.at[h], recv.at[11 + h])
        own = att_half[h, pl.ds(pl.multiple_of(spot * 8, 8), 8), :]
        att_mine[h] = (own + jnp.sum(att_slots[h], axis=0)) * grad_scale
        rows = at_rows(att_all.at[h], core * 512 + spot * 8, 8)
        pltpu.make_async_copy(att_mine.at[h], rows, recv.at[13 + h]).start()

        @pl.loop(1, 64)
        def _(k):
            remote(att_mine.at[h], rows, send.at[13 + h], recv.at[13 + h], same_core(k)).start()

    def att_swap_copy(h):
        rows = at_rows(att_all.at[h], core * 512, 512)
        return remote(rows, rows, send.at[22 + h], recv.at[22 + h], pair)

    def groups_range(h, first, count):
        @pl.loop(first // UNROLL_BACK, (first + count) // UNROLL_BACK)
        def _(b):
            groups_back(h, b)

    w_lanes = cat([wh, wh, wl], 1)

    def token_grads(g):
        cols = slice(8 * g, 8 * g + 8)
        d_gain = jnp.zeros((8, D), F32)
        d_shift = jnp.zeros((8, D), F32)
        for c in range(2):
            rows = slice(512 * c, 512 * c + 512)

            def part(block):
                return block.reshape(32, 16, -1)[:, cols].reshape(256, -1)

            dh, dl = split(cat([part(d_qkv[i, rows, :]) for i in range(6)], 1))
            dn = mm(cat([dh, dl, dh], 1), w_lanes, NT)
            unit = part(unit_s[rows, :])
            inverse = part(inverse_s[rows, :])[:, 0:1]
            d_x = norm_back(dn, unit, inverse, gain_one[...])
            d_grid[g, 4 * c : 4 * c + 4] = d_x.reshape(4, 8, 8, D)
            d_gain += fold_rows(dn * unit)
            d_shift += fold_rows(dn)

        sem = (15, 3)[g]
        pltpu.make_async_copy(d_grid.at[g, band], back.at[g, band], recv.at[sem]).start()

        @pl.loop(1, 8)
        def _(k):
            who = other_band(k)
            remote(d_grid.at[g, who], back.at[g, band], send.at[sem], recv.at[sem], who * 16 + lane).start()

        return d_gain, d_shift

    def att_step(h, n):
        if ATT_DIRECT[h]:
            return
        if n < 3:
            att_sums[h].scatter_finish(n - 1)
            att_sums[h].scatter_start(n)
        elif n == 3:
            att_sums[h].scatter_finish(2)
            att_sums[h].gather_start(2)
        else:
            att_sums[h].gather_finish(6 - n)
            att_sums[h].gather_start(5 - n)

    def att_finish(h):
        if ATT_DIRECT[h]:
            arrived(at_rows(att_all.at[h], core * 512, 512), recv.at[13 + h])
        else:
            att_sums[h].gather_finish(0)
        att_swap_copy(h).start()

    groups_range(0, 0, 8)
    ffn_scatter_finish(0)
    ffn_scatter_start(1)
    groups_range(0, 8, 8)
    ffn_scatter_finish(1)
    ffn_scatter_start(2)
    weight_grads(0)
    att_pair_copy(0).start()
    ffn_scatter_finish(2)
    ffn_gather_start(2)
    groups_range(1, 0, 8)
    ffn_gather_finish(2)
    ffn_gather_start(1)
    att_scatter_start(0)
    gain_0, shift_0 = token_grads(0)
    vec[6:7, :] = jnp.sum(gain_0, axis=0, keepdims=True)
    vec[7:8, :] = jnp.sum(shift_0, axis=0, keepdims=True)
    groups_range(1, 8, 8)
    ffn_gather_finish(1)
    ffn_gather_start(0)
    att_step(0, 1)
    gain_1, shift_1 = token_grads(1)
    vec[6:7, :] += jnp.sum(gain_1, axis=0, keepdims=True)
    vec[7:8, :] += jnp.sum(shift_1, axis=0, keepdims=True)
    vec_start(0, "core")
    att_step(0, 2)
    if ATT_DIRECT[0]:
        att_gather_start(0)
    weight_grads(1)
    att_pair_copy(1).start()
    vec[...] = vec_finish(0, "core")
    vec_start(1, "x")
    att_step(0, 3)
    att_scatter_start(1)
    att_step(0, 4)
    vec[...] = vec_finish(1, "x")
    vec_start(2, "y")
    att_step(1, 1)
    att_step(0, 5)
    vec[...] = vec_finish(2, "y")
    vec_start(3, "z")
    att_step(1, 2)
    if ATT_DIRECT[1]:
        att_gather_start(1)
    ffn_gather_finish(0)
    ffn_rows = at_rows(ffn_all, mine, 1024)
    ffn_swap = remote(ffn_rows, ffn_rows, send.at[20], recv.at[20], pair)
    ffn_swap.start()
    att_step(1, 3)
    att_step(1, 4)
    att_finish(0)
    vec_total[...] = vec_finish(3, "z") * grad_scale
    att_step(1, 5)
    att_finish(1)
    arrived(back.at[0], recv.at[15])
    arrived(back.at[1], recv.at[3])
    arrived(grid_tokens.at[0:7], send.at[0])
    arrived(grid_grad.at[0:7], send.at[1])
    for part in ffn_sums:
        part.drain()
    for h in range(2):
        if ATT_DIRECT[h]:
            arrived(att_slots.at[h], send.at[11 + h])
            arrived(att_slots.at[h], send.at[13 + h])
        else:
            att_sums[h].drain()
    arrived(d_grid.at[0, 0:7], send.at[15])
    arrived(d_grid.at[1, 0:7], send.at[3])
    ffn_swap.wait()
    att_swap_copy(0).wait()
    att_swap_copy(1).wait()


def finish_kernel(through, back, ffn_all, att_all, vec,
                  result, out_gain_one, out_shift_one, out_qkv, out_out, out_gain_two, out_shift_two, out_up, out_bias, out_down):
    for who in range(8):
        for g in range(2):
            cols = slice(16 * who + 8 * g, 16 * who + 8 * g + 8)
            result[:, cols, :] = through[:, cols, :] + back[g, who]
    out_gain_two[...] = vec[0:1, :]
    out_shift_two[...] = vec[1:2, :]
    out_gain_one[...] = vec[6:7, :]
    out_shift_one[...] = vec[7:8, :]
    for f in range(4):
        cols = slice(256 * f, 256 * f + 256)
        out_bias[:, cols] = vec[2 + f : 3 + f, :]
        out_up[:, cols] = jnp.transpose(ffn_all[cols, :])
        out_down[cols, :] = ffn_all[1024 + 256 * f : 1280 + 256 * f, :]
    for h in range(2):
        for n in range(3):
            out_qkv[:, 256 * n + 128 * h : 256 * n + 128 * h + 128] = att_all[h, 256 * n : 256 * n + 256, :]
        for n in range(2):
            out_out[128 * h : 128 * h + 128, 128 * n : 128 * n + 128] = att_all[h, 768 + 128 * n : 896 + 128 * n, :]


VM = pl.BlockSpec(memory_space=pltpu.VMEM)
HB = pl.BlockSpec(memory_space=pl.ANY)
LIMIT = 62 * 1024 * 1024


def shape(*dims):
    return jax.ShapeDtypeStruct(dims, F32)


def local(tokens, stored, upstream, drop_attn, drop_ffn, depth_keep, gain_one, shift_one, w_qkv, w_out,
          gain_two, shift_two, w_up, up_bias, w_down):
    def v(*dims):
        return pltpu.VMEM(dims, F32)

    def b(*dims):
        return pltpu.VMEM(dims, BF)

    parts = pl.pallas_call(
        kernel,
        out_shape=(shape(8, 128, D), shape(2, 8, 8, 8, D), shape(2048, D), shape(2, 1024, 128), shape(8, D)),
        in_specs=[HB] + [VM] * 14,
        out_specs=(VM,) * 5,
        scratch_shapes=[
            b(4, 256, 768), b(1024, 768), b(1024, 768),
            v(1024, 256), v(1024, 128), v(8, 128, D), v(8, 128, D), v(8, 128, D),
            v(8, 8, 16, D), v(8, 8, 16, D), v(2, 8, 8, 8, D),
            v(2048, D), v(1024, D), v(2, 3, 128, D), v(2, 3, 32, D), v(2, 3, 8, D), v(2, 3, 128, 128), v(2, 3, 32, 128), v(2, 3, 8, 128),
            v(2, 1024, 128), v(2, 512, 128), v(2, 63, 8, 128), v(2, 8, 128),
            v(8, D), v(4, 4, 8, D),
            v(6, 1024, 128), v(2, 16, 64, 256), v(2, 1024, 128), v(6, 1024, 128), v(2, 1024, 128),
            v(1024, 256), v(1024, 128), b(4, 256, 768), b(4, 768, 256),
            pltpu.SemaphoreType.DMA((48,)), pltpu.SemaphoreType.DMA((48,))],
        compiler_params=pltpu.CompilerParams(vmem_limit_bytes=LIMIT, collective_id=0, has_side_effects=True),
        name="block_back",
    )(tokens.reshape(8, 128, D), stored.reshape(8, 128, D), upstream.reshape(8, 128, D), drop_attn.transpose(1, 0, 2), drop_ffn.transpose(1, 0, 2), depth_keep,
      gain_one[None], shift_one[None], w_qkv, w_out, gain_two[None], shift_two[None], w_up, up_bias[None], w_down)
    outs = pl.pallas_call(
        finish_kernel,
        out_shape=(shape(8, 128, D), shape(1, D), shape(1, D), shape(D, 768), shape(D, D), shape(1, D), shape(1, D),
                   shape(D, FF), shape(1, FF), shape(FF, D)),
        in_specs=[VM] * 5,
        out_specs=(VM,) * 10,
        compiler_params=pltpu.CompilerParams(vmem_limit_bytes=LIMIT),
        name="finish",
    )(*parts)
    result, gain_one, shift_one, d_qkv, d_out, gain_two, shift_two, d_up, bias, d_down = outs
    return (result.reshape(1, 1024, D), gain_one[0], shift_one[0], d_qkv, d_out, gain_two[0], shift_two[0], d_up, bias[0], d_down)


def solution(mesh):
    banded = P("rows", None, None)
    return jax.shard_map(
        local,
        mesh=mesh,
        in_specs=(banded,) * 5 + (P(),) * 10,
        out_specs=(banded,) + (P(),) * 9,
        check_vma=False,
    )
```
